768 devices in a mesh: blk: 128 (over z_hi, y, x, core), group: 6 (over z_lo).
Axes of the slice: x: 4, y: 8, z: 12 (z_hi: 2, z_lo: 6; z = z_hi * 6 + z_lo), core: 2. Of those that a mesh axis runs over, the one named last changes fastest.
Arguments:
- aggregated_vision_descriptors: bfloat16 [98304, 1152], P(('blk', 'group')), may hold values from -24 to 24
- caption_vectors_unnormed: bfloat16 [98304, 1152], P(('blk', 'group')), may hold values from -0.19921875 to 0.19921875
- vision_projection_coefficients: bfloat16 [1152, 1152], replicated, may hold values from -0.1875 to 0.1875
- score_multiplier: float32 [1], replicated, may hold values from 5 to 15
- score_shift_term: float32 [1], replicated, may hold values from -3 to -1
Outputs:
- head_grad: bfloat16 [1152, 1152], P('blk')
- text_grad: bfloat16 [98304, 1152], P(('blk', 'group'))
The draws below stay inside these ranges and needn't reach their ends.
All inputs are finite; a program needn't handle non-finite values.
Results may differ from the reference program's by a relative error of at most 0.0095.
Values may be sent and summed in bfloat16 or wider, within the bound.
A program may use at most 32 MiB of HBM per device.

```python
import math
import jax
import jax.numpy as jnp
from jax import lax

D = 1152
ROWS = 128
TOKENS = 98304
N_BLK = 128
N_GROUP = 6


def with_spikes(drawn, key, source, target, parts, factor):
    owner, partner = [(jnp.arange(drawn.shape[dim]) // (drawn.shape[dim] // parts)).reshape([-1 if axis == dim else 1 for axis in range(drawn.ndim)]) for dim in (source, target)]
    chosen = jax.random.permutation(key, parts)[partner]
    strong = (owner == chosen) | (owner == (partner + parts // 2) % parts)
    return jnp.where(strong, factor * drawn, drawn)


def steps_of(rng, dims, split, smallest, high):
    gain, own = 1.0, jax.random.fold_in(rng, 6)
    for position, parts in split:
        heights = jnp.exp(jax.random.uniform(jax.random.fold_in(own, position), (parts,), jnp.float32, smallest / len(split), high / len(split)))
        gain = gain * jnp.repeat(heights, dims[position] // parts).reshape([-1 if axis == position else 1 for axis in range(len(dims))])
    return gain


def normal_values(rng, extent, spread, bound, split=(), kind=jnp.bfloat16):
    values = spread * jax.random.normal(rng, extent, jnp.float32)
    if split:
        values = values * steps_of(rng, extent, split, -0.22, 0.18)
    return jnp.clip(values, -bound, bound).astype(kind)


def heavy_noise(stream_key, shape, spread, most, pieces, heavy, kind=jnp.bfloat16):
    values = spread * jax.random.normal(stream_key, shape, jnp.float32)
    if pieces:
        values = values * steps_of(stream_key, shape, pieces, -0.22, 0.18)
    return jnp.clip(with_spikes(values, jax.random.fold_in(stream_key, 3), *heavy), -most, most).astype(kind)


def setup_inputs(seed: int = 0) -> dict:
    streams_of = jax.random.split(jax.random.key(seed), 6)
    return {
        "aggregated_vision_descriptors": heavy_noise(streams_of[0], (TOKENS, D), 1.0, 24.0, ((0, 768),), (0, 1, 384, 6.0)),
        "caption_vectors_unnormed": normal_values(streams_of[1], (TOKENS, D), 0.03, 0.19921875, ((0, 768),)),
        "vision_projection_coefficients": normal_values(streams_of[2], (D, D), D ** -0.5, 0.1875),
        "score_multiplier": jnp.clip(jnp.exp(jax.random.uniform(streams_of[3], (1,), jnp.float32, math.log(5.0), math.log(15.0))), 5.0, 15.0),
        "score_shift_term": jnp.clip(jax.random.uniform(streams_of[4], (1,), jnp.float32, -3.0, -1.0), -3.0, -1.0),
    }


epsilon = 1e-06

def reference(aggregated_vision_descriptors, caption_vectors_unnormed, vision_projection_coefficients, score_multiplier, score_shift_term):
    projected = jnp.dot(aggregated_vision_descriptors, vision_projection_coefficients, preferred_element_type=jnp.float32)
    img_inverse = lax.rsqrt(lax.optimization_barrier(jnp.sum(projected * projected, axis=1, keepdims=True)) + epsilon)
    unit_img = projected * img_inverse
    img_b = unit_img.astype(jnp.bfloat16)
    text_wide = caption_vectors_unnormed.astype(jnp.float32)
    txt_inverse = lax.rsqrt(lax.optimization_barrier(jnp.sum(text_wide * text_wide, axis=1, keepdims=True)) + epsilon)
    unit_txt = text_wide * txt_inverse
    txt_b = unit_txt.astype(jnp.bfloat16)
    picture_tile_sequence = img_b.reshape(N_BLK, N_GROUP, ROWS, D).astype(jnp.float32)
    txt_blocks = txt_b.reshape(N_BLK, N_GROUP, ROWS, D).astype(jnp.float32)
    positive = jnp.eye(ROWS, dtype=jnp.float32)
    image_grad = jnp.zeros((N_BLK, N_GROUP, ROWS, D), jnp.float32)
    text_sum = jnp.zeros((N_BLK, N_GROUP, ROWS, D), jnp.float32)
    offsets = ((0, 0), (1, 0), (1, 1), (2, 1))
    for blk_step, grp_step in offsets:
        counterpart_tile = jnp.roll(txt_blocks, (blk_step, grp_step), axis=(0, 1))
        match_scores = score_multiplier[0] * jnp.einsum('inxa,inua->inxu', picture_tile_sequence, counterpart_tile) + score_shift_term[0]
        projection_coefficients = jax.nn.sigmoid(match_scores)
        if blk_step == 0 and grp_step == 0:
            projection_coefficients = projection_coefficients - positive
        stretched_scores = (score_multiplier[0] * projection_coefficients).astype(jnp.bfloat16).astype(jnp.float32)
        image_grad = image_grad + jnp.einsum('bgij,bgjd->bgid', stretched_scores, counterpart_tile)
        piece = jnp.einsum('bgij,bgid->bgjd', stretched_scores, picture_tile_sequence)
        text_sum = text_sum + jnp.roll(piece, (-blk_step, -grp_step), axis=(0, 1))
    text_sum = text_sum.reshape(TOKENS, D)
    image_grad = image_grad.reshape(TOKENS, D)
    text_raw = (text_sum - unit_txt * lax.optimization_barrier(jnp.sum(unit_txt * text_sum, axis=1, keepdims=True))) * txt_inverse
    moved = jnp.roll(text_raw.reshape(N_BLK, N_GROUP, ROWS, D), (2, 1), axis=(0, 1)).reshape(TOKENS, D)
    text_grad = moved.astype(jnp.bfloat16)
    proj_grad = ((image_grad - unit_img * lax.optimization_barrier(jnp.sum(unit_img * image_grad, axis=1, keepdims=True))) * img_inverse).astype(jnp.bfloat16)
    head_grad = jnp.dot(aggregated_vision_descriptors.T, proj_grad, preferred_element_type=jnp.float32).astype(jnp.bfloat16)
    return (head_grad, text_grad)
```

```python
import jax
import jax.numpy as jnp
import numpy as np
from jax import lax
from jax.experimental import pallas as pl
from jax.experimental.pallas import tpu as pltpu
from jax.sharding import PartitionSpec as P

MESH = pl.DeviceIdType.MESH
EPS = 1e-06
NC, NX, NY, NZ, NG = 2, 4, 8, 12, 6
ROWS, D = 128, 1152
NT = D // 128
OWN = 9
BLOCK = 144
PIECE = 96
CHUNKS = 2
F32, BF16 = jnp.float32, jnp.bfloat16


def dot(a, b, ca=1, cb=0):
    return lax.dot_general(a, b, (((ca,), (cb,)), ((), ())), preferred_element_type=F32)


def unit_rows(wide):
    inverse = lax.rsqrt(jnp.sum(wide * wide, axis=1, keepdims=True) + EPS)
    return wide * inverse, inverse


def kernel(
    mult_ref, bias_ref, a_ref, t_ref, w_hbm, order_hbm,
    head_ref, tgrad_ref,
    w_ref, order_ref, proj_ref, img_ref, tx, ix, igrad, tsum,
    at_all, at_got, p_got, out, pieces, ysend, ygot, ysum, zsend, zgot, final,
    local_sem, t_ss, t_rs, i_ss, i_rs, a_ss, a_rs, p_ss, p_rs, q_ss, q_rs, y_ss, y_rs, z_ss, z_rs,
):
    b = lax.axis_index("blk")
    g = lax.axis_index("group")
    c, x, y, zh = b % 2, (b // 2) % NX, (b // 8) % NY, b // 64
    z = zh * NG + g

    def at(c_, x_, y_, z_):
        return ((z_ // NG) * 64 + y_ * 8 + x_ * 2 + c_, z_ % NG)

    after = ((b + 1) % 128, g)
    before = ((b + 127) % 128, g)
    up = (b, (g + 1) % NG)
    down = (b, (g + 5) % NG)
    partner = at(1 - c, x, y, z)

    load_w = pltpu.make_async_copy(w_hbm, w_ref, local_sem.at[0])
    load_w.start()
    load_order = pltpu.make_async_copy(order_hbm, order_ref, local_sem.at[1])
    load_order.start()

    ring = [at(core, (x + k) % NX, y, z) for k in range(1, NX) for core in range(NC)]
    column = [at(c, x, (y + k) % NY, z) for k in range(1, NY)]
    tower = [at(c, x, y, (z + k) % NZ) for k in range(1, NZ)]
    greeted = [after, before, up, down, partner] + ring + column + tower
    barrier = pltpu.get_barrier_semaphore()
    for device in greeted:
        pl.semaphore_signal(barrier, inc=1, device_id=device, device_id_type=MESH)
    pl.semaphore_wait(barrier, len(greeted))

    started = []

    def send(src, dst, ss, rs, device):
        copy = pltpu.make_async_remote_copy(
            src_ref=src, dst_ref=dst, send_sem=ss, recv_sem=rs, device_id=device, device_id_type=MESH
        )
        copy.start()
        started.append(copy)
        return copy

    def chunk(k):
        return pl.ds(k * (ROWS // CHUNKS), ROWS // CHUNKS)

    hop1 = [
        send(t_ref.at[chunk(k)], tx.at[0, chunk(k)], t_ss.at[0, k], t_rs.at[0, k], after)
        for k in range(CHUNKS)
    ]

    multiplier = mult_ref[0]
    bias = bias_ref[0]

    load_w.wait()
    for k in range(3):
        cols = pl.ds(k * 384, 384)
        proj_ref[:, cols] = dot(a_ref[...], w_ref[:, cols])
    unit, img_inverse = unit_rows(proj_ref[...])
    img_ref[...] = unit.astype(BF16)

    load_order.wait()
    for k in range(NX * NC):
        at_all[k] = dot(order_ref[pl.ds(k * BLOCK, BLOCK), :], a_ref[...], 1, 1).astype(BF16)
    at_got[0] = at_all[x * 2 + c]
    a_copies = []
    for k in range(NX):
        for dc in range(NC):
            slot = k * 2 + dc
            if slot == 0:
                continue
            tx_x, tx_c = (x + k) % NX, (c + dc) % 2
            a_copies.append(
                send(
                    at_all.at[tx_x * 2 + tx_c], at_got.at[slot], a_ss.at[slot], a_rs.at[slot],
                    at(tx_c, tx_x, y, z),
                )
            )

    def txt_of(raw):
        return unit_rows(raw.astype(F32))[0].astype(BF16)

    rows = lax.broadcasted_iota(jnp.int32, (ROWS, ROWS), 0)
    cols = lax.broadcasted_iota(jnp.int32, (ROWS, ROWS), 1)
    positive = jnp.where(rows == cols, 1.0, 0.0).astype(F32)

    def scaled_of(left, right, own):
        logits = multiplier * dot(left, right, 1, 1) + bias
        weight = jax.nn.sigmoid(logits)
        if own:
            weight = weight - positive
        return (multiplier * weight).astype(BF16)

    def image_pair(raw, own):
        txt_b = txt_of(raw)
        term = dot(scaled_of(img_ref[...], txt_b, own), txt_b)
        if own:
            igrad[...] = term
        else:
            igrad[...] += term

    hop2 = []
    for k in range(CHUNKS):
        hop1[k].wait_recv()
        hop2.append(send(tx.at[0, chunk(k)], tx.at[1, chunk(k)], t_ss.at[1, k], t_rs.at[1, k], up))
    image_pair(t_ref[...], True)
    image_pair(tx[0], False)
    hop3 = []
    for k in range(CHUNKS):
        hop2[k].wait_recv()
        hop3.append(send(tx.at[1, chunk(k)], tx.at[2, chunk(k)], t_ss.at[2, k], t_rs.at[2, k], after))
    image_pair(tx[1], False)
    for k in range(CHUNKS):
        hop3[k].wait_recv()
    image_pair(tx[2], False)

    unit, img_inverse = unit_rows(proj_ref[...])
    grad = igrad[...]
    p_got[0] = (
        (grad - unit * jnp.sum(unit * grad, axis=1, keepdims=True)) * img_inverse
    ).astype(BF16)

    p_copies = {}
    for k in (2, 1, 3):
        p_copies[k] = send(
            p_got.at[0], p_got.at[k * 2], p_ss.at[k], p_rs.at[k], at(c, (x + k) % NX, y, z)
        )
    q_copies = {0: send(p_got.at[0], p_got.at[1], q_ss.at[0], q_rs.at[0], partner)}
    i_hop1 = send(img_ref, ix.at[0], i_ss.at[0], i_rs.at[0], after)

    for copy in a_copies:
        copy.wait_recv()
    out[...] = dot(at_got[0], p_got[0])
    for k in (1, 3, 2):
        p_copies[k].wait_recv()
        q_copies[k] = send(p_got.at[k * 2], p_got.at[k * 2 + 1], q_ss.at[k], q_rs.at[k], partner)
        out[...] += dot(at_got[k * 2], p_got[k * 2])
    for k in (0, 1, 3, 2):
        q_copies[k].wait_recv()
        out[...] += dot(at_got[k * 2 + 1], p_got[k * 2 + 1])

    for q in range(NY):
        for half in range(2):
            for j in range(NT):
                source = (q * 2 + half) * OWN
                target = half * PIECE + j * OWN
                pieces[q, target : target + OWN, :] = out[source : source + OWN, j * 128 : (j + 1) * 128]
            pad = half * PIECE + NT * OWN
            pieces[q, pad : (half + 1) * PIECE, :] = jnp.zeros((PIECE - NT * OWN, 128), F32)
    ysend[...] = pieces[...].astype(BF16)
    y_copies = []
    for k in (4, 3, 5, 2, 6, 1, 7):
        to_y = (y + k) % NY
        y_copies.append(send(ysend.at[to_y], ygot.at[k], y_ss.at[k], y_rs.at[k], at(c, x, to_y, z)))

    i_hop1.wait_recv()
    i_hop2 = send(ix.at[0], ix.at[1], i_ss.at[1], i_rs.at[1], up)

    total = pieces[y]
    for k, copy in zip((4, 3, 5, 2, 6, 1, 7), y_copies):
        copy.wait_recv()
        total = total + ygot[k].astype(F32)
    zsend[0] = total[:PIECE].astype(BF16)
    zsend[1] = total[PIECE:].astype(BF16)
    zgot[z] = zsend[zh]
    z_copies = []
    for k in (6, 5, 7, 4, 8, 3, 9, 2, 10, 1, 11):
        to_z = (z + k) % NZ
        z_copies.append(
            send(zsend.at[to_z // NG], zgot.at[z], z_ss.at[k], z_rs.at[k], at(c, x, y, to_z))
        )

    i_hop2.wait_recv()
    i_hop3 = send(ix.at[1], ix.at[2], i_ss.at[2], i_rs.at[2], after)

    unit_txt, txt_inverse = unit_rows(tx[2].astype(F32))
    txt_b = unit_txt.astype(BF16)

    def text_pair(image, own):
        return dot(scaled_of(txt_b, image, own), image)

    tsum[...] = text_pair(img_ref[...], False)
    tsum[...] += text_pair(ix[0], False)
    tsum[...] += text_pair(ix[1], False)

    for k, copy in zip((6, 5, 7, 4, 8, 3, 9, 2, 10, 1, 11), z_copies):
        copy.wait_recv()
    total = zgot[0].astype(F32)
    for k in range(1, NZ):
        total = total + zgot[k].astype(F32)
    final[...] = total
    for j in range(NT):
        head_ref[:, j * 128 : (j + 1) * 128] = final[j * OWN : (j + 1) * OWN, :].astype(BF16)

    i_hop3.wait_recv()
    tsum[...] += text_pair(ix[2], True)
    grad = tsum[...]
    unit_txt, txt_inverse = unit_rows(tx[2].astype(F32))
    tgrad_ref[...] = (
        (grad - unit_txt * jnp.sum(unit_txt * grad, axis=1, keepdims=True)) * txt_inverse
    ).astype(BF16)

    for copy in started:
        copy.wait_send()


def row_order():
    source = np.arange(D).reshape(2, NY, NX, NC, OWN).transpose(2, 3, 1, 0, 4).reshape(-1)
    order = np.zeros((D, D), np.float32)
    order[np.arange(D), source] = 1.0
    return order


def local(descriptors, captions, weights, multiplier, bias):
    order = jnp.asarray(row_order(), BF16)
    vmem = pl.BlockSpec(memory_space=pltpu.VMEM)
    smem = pl.BlockSpec(memory_space=pltpu.SMEM)
    hbm = pl.BlockSpec(memory_space=pl.ANY)
    dma = pltpu.SemaphoreType.DMA
    head, text = pl.pallas_call(
        kernel,
        out_shape=(
            jax.ShapeDtypeStruct((OWN, D), BF16),
            jax.ShapeDtypeStruct((ROWS, D), BF16),
        ),
        in_specs=[smem, smem, vmem, vmem, hbm, hbm],
        out_specs=(vmem, vmem),
        scratch_shapes=[
            pltpu.VMEM((D, D), BF16),
            pltpu.VMEM((D, D), BF16),
            pltpu.VMEM((ROWS, D), F32),
            pltpu.VMEM((ROWS, D), BF16),
            pltpu.VMEM((3, ROWS, D), BF16),
            pltpu.VMEM((3, ROWS, D), BF16),
            pltpu.VMEM((ROWS, D), F32),
            pltpu.VMEM((ROWS, D), F32),
            pltpu.VMEM((NX * NC, BLOCK, ROWS), BF16),
            pltpu.VMEM((NX * NC, BLOCK, ROWS), BF16),
            pltpu.VMEM((NX * NC, ROWS, D), BF16),
            pltpu.VMEM((BLOCK, D), F32),
            pltpu.VMEM((NY, 2 * PIECE, 128), F32),
            pltpu.VMEM((NY, 2 * PIECE, 128), BF16),
            pltpu.VMEM((NY, 2 * PIECE, 128), BF16),
            pltpu.VMEM((2 * PIECE, 128), F32),
            pltpu.VMEM((2, PIECE, 128), BF16),
            pltpu.VMEM((NZ, PIECE, 128), BF16),
            pltpu.VMEM((PIECE, 128), F32),
            dma((2,)),
            dma((3, CHUNKS)),
            dma((3, CHUNKS)),
            dma((3,)),
            dma((3,)),
            dma((NX * NC,)),
            dma((NX * NC,)),
            dma((NX,)),
            dma((NX,)),
            dma((NX,)),
            dma((NX,)),
            dma((NY,)),
            dma((NY,)),
            dma((NZ,)),
            dma((NZ,)),
        ],
        compiler_params=pltpu.CompilerParams(
            collective_id=0, has_side_effects=True, vmem_limit_bytes=48 * 1024 * 1024
        ),
        name="window_grads",
    )(multiplier, bias, descriptors, captions, weights, order)
    return head, text


def solution(mesh):
    in_specs = (P(("blk", "group"), None), P(("blk", "group"), None), P(), P(), P())
    out_specs = (P("blk", None), P(("blk", "group"), None))
    return jax.shard_map(local, mesh=mesh, in_specs=in_specs, out_specs=out_specs, check_vma=False)
```

```python
import jax
import jax.numpy as jnp
import numpy as np
from jax import lax
from jax.experimental import pallas as pl
from jax.experimental.pallas import tpu as pltpu
from jax.sharding import PartitionSpec as P

MESH = pl.DeviceIdType.MESH
EPS = 1e-06
NC, NX, NY, NZ, NG = 2, 4, 8, 12, 6
ROWS, D = 128, 1152
OWN = 9
BLOCK = 144
COLS = 384
PARTS = 3
PIECE = 32
CHUNKS = 4
NT = COLS // 128
SLICE = ROWS // CHUNKS
HALF = ROWS // 2
F32, BF16 = jnp.float32, jnp.bfloat16


def dot(a, b, ca=1, cb=0):
    return lax.dot_general(a, b, (((ca,), (cb,)), ((), ())), preferred_element_type=F32)


def unit_rows(wide):
    inverse = lax.rsqrt(jnp.sum(wide * wide, axis=1, keepdims=True) + EPS)
    return wide * inverse, inverse


def kernel(
    mult_ref, bias_ref, a_hbm, t_hbm, w_hbm, order_hbm,
    head_ref, tgrad_ref,
    a_ref, t_ref, w_ref, order_ref, proj_ref, img_ref, tx, ix, relayed, igrad, tsum,
    at_all, at_got, p_got, out, pieces, ysend, ygot, zsend, zgot, final,
    local_sem, t_ss, t_rs, i_ss, i_rs, r_ss, r_rs, a_ss, a_rs,
    p_ss, p_rs, f_ss, q_ss, q_rs, y_ss, y_rs, z_ss, z_rs,
):
    b = lax.axis_index("blk")
    g = lax.axis_index("group")
    c, x, y, zh = b % 2, (b // 2) % NX, (b // 8) % NY, b // 64
    z = zh * NG + g

    def at(c_, x_, y_, z_):
        return ((z_ // NG) * 64 + y_ * 8 + x_ * 2 + c_, z_ % NG)

    after = ((b + 1) % 128, g)
    before = ((b + 127) % 128, g)
    up = (b, (g + 1) % NG)
    down = (b, (g + 5) % NG)
    partner = at(1 - c, x, y, z)
    right = at(c, (x + 1) % NX, y, z)
    left = at(c, (x + 3) % NX, y, z)

    far_z = (z + 6) % NZ
    is_source = (c == 1) & (x == 3) & (y == 7)
    is_target = (c == 0) & (x == 0) & (y == 0)
    is_relay = (c == 1) & (((x == 0) & (y == 7)) | ((x == 3) & (y == 0)) | ((x == 0) & (y == 0)))
    relay_chunk = jnp.where(y == 7, 1, jnp.where(x == 3, 2, 3))

    def relays_at(z_):
        return [None, at(1, 0, 7, z_), at(1, 3, 0, z_), at(1, 0, 0, z_)]

    loads = []
    for i, (src, dst) in enumerate(
        ((t_hbm, t_ref), (a_hbm, a_ref), (w_hbm, w_ref), (order_hbm, order_ref))
    ):
        load = pltpu.make_async_copy(src, dst, local_sem.at[i])
        load.start()
        loads.append(load)

    ring = [at(core, (x + k) % NX, y, z) for k in range(1, NX) for core in range(NC)]
    column = [at(c, x, (y + k) % NY, z) for k in range(1, NY)]
    tower = [at(c, x, y, (z + k) % NZ) for k in range(1, NZ)]
    greeted = [after, before, up, down, partner] + ring + column + tower
    barrier = pltpu.get_barrier_semaphore()

    def greet(device):
        pl.semaphore_signal(barrier, inc=1, device_id=device, device_id_type=MESH)

    for device in greeted:
        greet(device)

    @pl.when(is_source)
    def _():
        for device in relays_at(z)[1:]:
            greet(device)

    @pl.when(is_relay)
    def _():
        greet(at(1, 3, 7, z))
        greet(at(0, 0, 0, far_z))

    @pl.when(is_target)
    def _():
        for device in relays_at(far_z)[1:]:
            greet(device)

    loads[0].wait()
    ends = is_source.astype(jnp.int32) + is_target.astype(jnp.int32)
    pl.semaphore_wait(barrier, len(greeted) + 3 * ends + 2 * is_relay.astype(jnp.int32))

    started = []

    def remote(src, dst, ss, rs, device):
        return pltpu.make_async_remote_copy(
            src_ref=src, dst_ref=dst, send_sem=ss, recv_sem=rs, device_id=device, device_id_type=MESH
        )

    def send(src, dst, ss, rs, device):
        copy = remote(src, dst, ss, rs, device)
        copy.start()
        started.append(copy)
        return copy

    def chunk(k):
        return pl.ds(k * SLICE, SLICE)

    def send_after(src, dst, kind, ss, rs, k):
        direct = remote(src, dst, ss, rs, after)
        started.append(direct)
        if k == 0:
            direct.start()
        else:
            @pl.when(is_source)
            def _():
                remote(src, relayed.at[kind], ss, r_rs.at[kind], relays_at(z)[k]).start()

            @pl.when(jnp.logical_not(is_source))
            def _():
                direct.start()
        return direct

    def relay_copy(kind, dst, rs):
        piece = pl.ds(pl.multiple_of(relay_chunk * SLICE, SLICE), SLICE)
        return remote(
            relayed.at[kind], dst.at[piece], r_ss.at[kind], rs.at[relay_chunk], at(0, 0, 0, far_z)
        )

    def relay(kind, dst, rs):
        @pl.when(is_relay)
        def _():
            remote(relayed.at[kind], relayed.at[kind], r_ss.at[kind], r_rs.at[kind], after).wait_recv()
            relay_copy(kind, dst, rs).start()

    def relay_end(kind, dst, rs):
        @pl.when(is_relay)
        def _():
            relay_copy(kind, dst, rs).wait_send()

    def text_hop(hop, k, source):
        return (source.at[chunk(k)], tx.at[hop, chunk(k)], t_ss.at[hop, k], t_rs.at[hop, k])

    def image_hop(hop, k, source):
        return (source.at[chunk(k)], ix.at[hop, chunk(k)], i_ss.at[hop, k], i_rs.at[hop, k])

    def after_hop(args, kind, k):
        src, dst, ss, rs = args
        return send_after(src, dst, kind, ss, rs, k)

    hop1 = [after_hop(text_hop(0, k, t_ref), 0, k) for k in range(CHUNKS)]

    loads[1].wait()
    loads[2].wait()
    for k in range(3):
        cols = pl.ds(k * 384, 384)
        proj_ref[:, cols] = dot(a_ref[...], w_ref[:, cols])
    unit, img_inverse = unit_rows(proj_ref[...])
    img_ref[...] = unit.astype(BF16)
    i_hop1 = [after_hop(image_hop(0, k, img_ref), 1, k) for k in range(CHUNKS)]

    multiplier = mult_ref[0]
    bias = bias_ref[0]

    def txt_of(raw):
        return unit_rows(raw.astype(F32))[0].astype(BF16)

    rows = lax.broadcasted_iota(jnp.int32, (ROWS, ROWS), 0)
    cols = lax.broadcasted_iota(jnp.int32, (ROWS, ROWS), 1)
    positive = jnp.where(rows == cols, 1.0, 0.0).astype(F32)

    def scaled_of(left_rows, right_rows, own):
        logits = multiplier * dot(left_rows, right_rows, 1, 1) + bias
        weight = jax.nn.sigmoid(logits)
        if own:
            weight = weight - positive
        return (multiplier * weight).astype(BF16)

    def image_pair(raw, own):
        txt_b = txt_of(raw)
        term = dot(scaled_of(img_ref[...], txt_b, own), txt_b)
        if own:
            igrad[...] = term
        else:
            igrad[...] += term

    hop2 = []
    for k in range(CHUNKS):
        hop1[k].wait_recv()
        hop2.append(send(*text_hop(1, k, tx.at[0]), up))
    relay(0, tx.at[0], t_rs.at[0])
    loads[3].wait()
    for k in range(NX * NC):
        at_all[k] = dot(order_ref[pl.ds(k * BLOCK, BLOCK), :], a_ref[...], 1, 1).astype(BF16)
    at_got[0, :, :128] = at_all[x * 2 + c]
    a_copies = []
    for k in range(NX):
        for dc in range(NC):
            slot = k * 2 + dc
            if slot == 0:
                continue
            to_x, to_c = (x + k) % NX, (c + dc) % 2
            a_copies.append(
                send(
                    at_all.at[to_x * 2 + to_c], at_got.at[k, :, pl.ds(dc * 128, 128)],
                    a_ss.at[slot], a_rs.at[slot], at(to_c, to_x, y, z),
                )
            )
    image_pair(t_ref[...], True)
    image_pair(tx[0], False)
    for q in range(PARTS):
        for half in range(2):
            pieces[q, :, half * PIECE + NT * OWN : (half + 1) * PIECE, :] = jnp.zeros(
                (NY, PIECE - NT * OWN, 128), F32
            )
    relay(1, ix.at[0], i_rs.at[0])
    hop3 = []
    for k in range(CHUNKS):
        hop2[k].wait_recv()
        hop3.append(after_hop(text_hop(2, k, tx.at[1]), 2, k))
    relay(2, tx.at[2], t_rs.at[2])
    image_pair(tx[1], False)
    i_hop2 = []
    for k in range(CHUNKS):
        i_hop1[k].wait_recv()
        i_hop2.append(send(*image_hop(1, k, ix.at[0]), up))
    for k in range(CHUNKS):
        hop3[k].wait_recv()
    image_pair(tx[2], False)

    unit, img_inverse = unit_rows(proj_ref[...])
    grad = igrad[...]
    proj_grad = (
        (grad - unit * jnp.sum(unit * grad, axis=1, keepdims=True)) * img_inverse
    ).astype(BF16)
    for q in range(PARTS):
        p_got[0, q, :ROWS] = proj_grad[:, q * COLS : (q + 1) * COLS]

    first, second = pl.ds(0, HALF), pl.ds(HALF, HALF)
    own_rows, partner_rows = pl.ds(0, ROWS), pl.ds(ROWS, ROWS)
    p_copies, q_copies, f_copies, y_copies = {}, {}, {}, {}

    def p_send(k, q, half, device):
        rows_ = (first, second)[half]
        p_copies[k, q, half] = send(
            p_got.at[0, q, rows_], p_got.at[k, q, rows_], p_ss.at[k, q, half], p_rs.at[k, q, half], device
        )

    def q_send(k, q):
        q_copies[k, q] = send(
            p_got.at[k, q, own_rows], p_got.at[k, q, partner_rows], q_ss.at[k, q], q_rs.at[k, q], partner
        )

    for q in range(PARTS):
        p_send(1, q, 0, right)
        p_send(3, q, 1, left)
        p_send(1, q, 1, right)
        p_send(3, q, 0, left)
    for q in range(PARTS):
        q_send(0, q)

    def forward(q):
        p_copies[1, q, 0].wait_recv()
        f_copies[q, 0] = send(
            p_got.at[1, q, first], p_got.at[2, q, first], f_ss.at[q, 0], p_rs.at[2, q, 0], right
        )
        p_copies[3, q, 1].wait_recv()
        f_copies[q, 1] = send(
            p_got.at[3, q, second], p_got.at[2, q, second], f_ss.at[q, 1], p_rs.at[2, q, 1], left
        )

    def over_x(q):
        p_copies[1, q, 1].wait_recv()
        q_send(1, q)
        p_copies[3, q, 0].wait_recv()
        q_send(3, q)
        f_copies[q, 0].wait_recv()
        f_copies[q, 1].wait_recv()
        q_send(2, q)
        for k in range(NX):
            q_copies[k, q].wait_recv()
        acc = dot(at_got[0], p_got[0, q])
        for k in range(1, NX):
            acc = acc + dot(at_got[k], p_got[k, q])
        out[...] = acc
        for to_y in range(NY):
            for half in range(2):
                for j in range(NT):
                    source = (to_y * 2 + half) * OWN
                    target = half * PIECE + j * OWN
                    pieces[q, to_y, target : target + OWN, :] = out[
                        source : source + OWN, j * 128 : (j + 1) * 128
                    ]
        ysend[q] = pieces[q].astype(BF16)
        for k in (4, 3, 5, 2, 6, 1, 7):
            to_y = (y + k) % NY
            y_copies[q, k] = send(
                ysend.at[q, to_y], ygot.at[q, k], y_ss.at[q, k], y_rs.at[q, k], at(c, x, to_y, z)
            )

    z_copies = {}

    def over_y(q):
        total = pieces[q, y]
        for k in (1, 7, 2, 6, 3, 5, 4):
            y_copies[q, k].wait_recv()
            total = total + ygot[q, k].astype(F32)
        zsend[q, 0] = total[:PIECE].astype(BF16)
        zsend[q, 1] = total[PIECE:].astype(BF16)
        zgot[q, z] = zsend[q, zh]
        for k in (6, 5, 7, 4, 8, 3, 9, 2, 10, 1, 11):
            to_z = (z + k) % NZ
            z_copies[q, k] = send(
                zsend.at[q, to_z // NG], zgot.at[q, z], z_ss.at[q, k], z_rs.at[q, k], at(c, x, y, to_z)
            )

    for copy in a_copies:
        copy.wait_recv()
    forward(0)
    forward(1)
    over_x(0)
    forward(2)
    i_hop3 = []
    for k in range(CHUNKS):
        i_hop2[k].wait_recv()
        i_hop3.append(after_hop(image_hop(2, k, ix.at[1]), 3, k))
    over_x(1)
    relay(3, ix.at[2], i_rs.at[2])
    over_y(0)
    over_x(2)
    over_y(1)
    over_y(2)

    txt_b = txt_of(tx[2])

    def text_pair(image, own):
        return dot(scaled_of(txt_b, image, own), image)

    tsum[...] = text_pair(img_ref[...], False)
    tsum[...] += text_pair(ix[0], False)
    tsum[...] += text_pair(ix[1], False)

    for k in range(CHUNKS):
        i_hop3[k].wait_recv()
    tsum[...] += text_pair(ix[2], True)
    grad = tsum[...]
    unit_txt, txt_inverse = unit_rows(tx[2].astype(F32))
    tgrad_ref[...] = (
        (grad - unit_txt * jnp.sum(unit_txt * grad, axis=1, keepdims=True)) * txt_inverse
    ).astype(BF16)

    for q in range(PARTS):
        for k in (1, 11, 2, 10, 3, 9, 4, 8, 5, 7, 6):
            z_copies[q, k].wait_recv()
        total = zgot[q, 0].astype(F32)
        for k in range(1, NZ):
            total = total + zgot[q, k].astype(F32)
        final[...] = total
        for j in range(NT):
            target = (q * NT + j) * 128
            head_ref[:, target : target + 128] = final[j * OWN : (j + 1) * OWN, :].astype(BF16)

    for copy in started:
        copy.wait_send()
    relay_end(0, tx.at[0], t_rs.at[0])
    relay_end(1, ix.at[0], i_rs.at[0])
    relay_end(2, tx.at[2], t_rs.at[2])
    relay_end(3, ix.at[2], i_rs.at[2])


def row_order():
    source = np.arange(D).reshape(2, NY, NX, NC, OWN).transpose(2, 3, 1, 0, 4).reshape(-1)
    order = np.zeros((D, D), np.float32)
    order[np.arange(D), source] = 1.0
    return order


def local(descriptors, captions, weights, multiplier, bias):
    order = jnp.asarray(row_order(), BF16)
    vmem = pl.BlockSpec(memory_space=pltpu.VMEM)
    smem = pl.BlockSpec(memory_space=pltpu.SMEM)
    hbm = pl.BlockSpec(memory_space=pltpu.HBM)
    dma = pltpu.SemaphoreType.DMA
    head, text = pl.pallas_call(
        kernel,
        out_shape=(
            jax.ShapeDtypeStruct((OWN, D), BF16),
            jax.ShapeDtypeStruct((ROWS, D), BF16),
        ),
        in_specs=[smem, smem, hbm, hbm, hbm, hbm],
        out_specs=(vmem, vmem),
        scratch_shapes=[
            pltpu.VMEM((ROWS, D), BF16),
            pltpu.VMEM((ROWS, D), BF16),
            pltpu.VMEM((D, D), BF16),
            pltpu.VMEM((D, D), BF16),
            pltpu.VMEM((ROWS, D), F32),
            pltpu.VMEM((ROWS, D), BF16),
            pltpu.VMEM((3, ROWS, D), BF16),
            pltpu.VMEM((3, ROWS, D), BF16),
            pltpu.VMEM((4, SLICE, D), BF16),
            pltpu.VMEM((ROWS, D), F32),
            pltpu.VMEM((ROWS, D), F32),
            pltpu.VMEM((NX * NC, BLOCK, ROWS), BF16),
            pltpu.VMEM((NX, BLOCK, NC * ROWS), BF16),
            pltpu.VMEM((NX, PARTS, NC * ROWS, COLS), BF16),
            pltpu.VMEM((BLOCK, COLS), F32),
            pltpu.VMEM((PARTS, NY, 2 * PIECE, 128), F32),
            pltpu.VMEM((PARTS, NY, 2 * PIECE, 128), BF16),
            pltpu.VMEM((PARTS, NY, 2 * PIECE, 128), BF16),
            pltpu.VMEM((PARTS, 2, PIECE, 128), BF16),
            pltpu.VMEM((PARTS, NZ, PIECE, 128), BF16),
            pltpu.VMEM((PIECE, 128), F32),
            dma((4,)),
            dma((3, CHUNKS)),
            dma((3, CHUNKS)),
            dma((3, CHUNKS)),
            dma((3, CHUNKS)),
            dma((4,)),
            dma((4,)),
            dma((NX * NC,)),
            dma((NX * NC,)),
            dma((NX, PARTS, 2)),
            dma((NX, PARTS, 2)),
            dma((PARTS, 2)),
            dma((NX, PARTS)),
            dma((NX, PARTS)),
            dma((PARTS, NY)),
            dma((PARTS, NY)),
            dma((PARTS, NZ)),
            dma((PARTS, NZ)),
        ],
        compiler_params=pltpu.CompilerParams(
            collective_id=0, has_side_effects=True, vmem_limit_bytes=60 * 1024 * 1024
        ),
        name="window_grads",
    )(multiplier, bias, descriptors, captions, weights, order)
    return head, text


def solution(mesh):
    in_specs = (P(("blk", "group"), None), P(("blk", "group"), None), P(), P(), P())
    out_specs = (P("blk", None), P(("blk", "group"), None))
    return jax.shard_map(local, mesh=mesh, in_specs=in_specs, out_specs=out_specs, check_vma=False)
```

```python
import jax
import jax.numpy as jnp
import numpy as np
from jax import lax
from jax.experimental import pallas as pl
from jax.experimental.pallas import tpu as pltpu
from jax.sharding import PartitionSpec as P

MESH = pl.DeviceIdType.MESH
EPS = 1e-06
NC, NX, NY, NZ, NG = 2, 4, 8, 12, 6
ROWS, D = 128, 1152
OWN = 9
BLOCK = 144
COLS = 384
PARTS = 3
PIECE = 32
CHUNKS = 4
NT = COLS // 128
SLICE = ROWS // CHUNKS
HALF = ROWS // 2
RELAYS = ((0, 3, 7), (1, 0, 7), (1, 3, 0), (1, 0, 0), (1, 2, 7), (1, 2, 0), (1, 3, 6), (1, 0, 6))
STRIP = ROWS // len(RELAYS)
F32, BF16 = jnp.float32, jnp.bfloat16


def dot(a, b, ca=1, cb=0):
    return lax.dot_general(a, b, (((ca,), (cb,)), ((), ())), preferred_element_type=F32)


def unit_rows(wide):
    inverse = lax.rsqrt(jnp.sum(wide * wide, axis=1, keepdims=True) + EPS)
    return wide * inverse, inverse


def kernel(
    mult_ref, bias_ref, a_hbm, t_hbm, w_hbm, order_hbm,
    head_ref, tgrad_ref,
    a_ref, t_ref, w_ref, order_ref, proj_ref, img_ref, tx, ix, relayed, igrad, tsum,
    at_all, at_got, p_got, out, pieces, ysend, ygot, zsend, zgot, final,
    near_y, mid_y, near_z, mid_z, far_sem, local_sem, s_ss, t_ss, t_rs, i_ss, i_rs, r_ss, r_rs, a_ss, a_rs,
    p_ss, p_rs, f_ss, q_ss, q_rs, y_ss, y_rs, z_ss, z_rs,
):
    b = lax.axis_index("blk")
    g = lax.axis_index("group")
    c, x, y, zh = b % 2, (b // 2) % NX, (b // 8) % NY, b // 64
    z = zh * NG + g

    def at(c_, x_, y_, z_):
        return ((z_ // NG) * 64 + y_ * 8 + x_ * 2 + c_, z_ % NG)

    after = ((b + 1) % 128, g)
    before = ((b + 127) % 128, g)
    up = (b, (g + 1) % NG)
    down = (b, (g + 5) % NG)
    partner = at(1 - c, x, y, z)
    right = at(c, (x + 1) % NX, y, z)
    left = at(c, (x + 3) % NX, y, z)

    far_z = (z + 6) % NZ
    is_source = (c == 1) & (x == 3) & (y == 7)
    is_target = (c == 0) & (x == 0) & (y == 0)
    is_second = (c == 0) & (x == 3) & (y == 7)
    place = (y * NX + x) * NC + c
    is_third, relay_strip = b < 0, 0
    for i, (c_, x_, y_) in enumerate(RELAYS):
        here = place == (y_ * NX + x_) * NC + c_
        if i:
            is_third = is_third | here
        relay_strip = relay_strip + i * here.astype(jnp.int32)
    is_relay = is_second | is_third
    other = (1 - zh) * NG
    target_z = (far_z, other + (g + 1) % NG)
    origin_z = (far_z, other + (g + 5) % NG)

    def relays_at(z_):
        return [at(*spot, z_) for spot in RELAYS]

    loads = []
    for i, (src, dst) in enumerate(
        ((t_hbm, t_ref), (a_hbm, a_ref), (w_hbm, w_ref), (order_hbm, order_ref))
    ):
        load = pltpu.make_async_copy(src, dst, local_sem.at[i])
        load.start()
        loads.append(load)

    ring = [at(core, (x + k) % NX, y, z) for k in range(1, NX) for core in range(NC)]
    column = [at(c, x, (y + k) % NY, z) for k in (1, 7)]
    tower = [at(c, x, y, (z + k) % NZ) for k in (1, 11)]
    greeted = [up, down, partner] + ring + column + tower
    barrier = pltpu.get_barrier_semaphore()

    def greet(device):
        pl.semaphore_signal(barrier, inc=1, device_id=device, device_id_type=MESH)

    for device in greeted:
        greet(device)

    @pl.when(jnp.logical_not(is_source))
    def _():
        greet(after)

    @pl.when(jnp.logical_not(is_target))
    def _():
        greet(before)

    @pl.when(is_relay)
    def _():
        greet(at(1, 3, 7, z))

    @pl.when(is_third)
    def _():
        greet(at(0, 3, 7, z))

    @pl.when(is_target)
    def _():
        for z_ in origin_z:
            for device in relays_at(z_):
                greet(device)

    loads[0].wait()
    def one(flag):
        return flag.astype(jnp.int32)

    expected = len(greeted) + 2 + (len(RELAYS) - 1) * one(is_source) - one(is_target)
    expected = expected + 2 * one(is_relay) + (len(RELAYS) - 1) * one(is_second)
    pl.semaphore_wait(barrier, expected)

    def tell(sem, devices):
        for device in devices:
            pl.semaphore_signal(sem, inc=1, device_id=device, device_id_type=MESH)

    two_column = [at(c, x, (y + k) % NY, z) for k in (2, 6)]
    two_tower = [at(c, x, y, (z + k) % NZ) for k in (2, 10)]
    tell(near_y, column)
    tell(near_z, tower)

    started, kept = [], []

    def remote(src, dst, ss, rs, device):
        return pltpu.make_async_remote_copy(
            src_ref=src, dst_ref=dst, send_sem=ss, recv_sem=rs, device_id=device, device_id_type=MESH
        )

    def send(src, dst, ss, rs, device):
        copy = remote(src, dst, ss, rs, device)
        copy.start()
        started.append(copy)
        return copy

    def strip(i):
        return pl.ds(i * STRIP, STRIP)

    def chunk(k):
        return pl.ds(k * SLICE, SLICE)

    def send_after(src, dst, kind, ss, rs, k, whole):
        direct = remote(src, dst, ss, rs, after)
        if kind >= 2:
            kept.append(direct)
        else:
            started.append(direct)

            @pl.when(is_source)
            def _():
                for i in range(k * SLICE // STRIP, (k + 1) * SLICE // STRIP):
                    remote(
                        whole.at[strip(i)], relayed.at[kind], ss, r_rs.at[kind], relays_at(z)[i]
                    ).start()

        @pl.when(jnp.logical_not(is_source))
        def _():
            direct.start()

        return direct

    def second_copies(src, kind):
        return [
            remote(src.at[strip(i)], relayed.at[kind], s_ss.at[kind - 2, i], r_rs.at[kind], relays_at(z)[i])
            for i in range(1, len(RELAYS))
        ]

    def second_start(src, kind):
        @pl.when(is_second)
        def _():
            for copy in second_copies(src, kind):
                copy.start()

    def second_end(src, kind):
        @pl.when(is_second)
        def _():
            for copy in second_copies(src, kind):
                copy.wait_send()

    def relay_copy(kind, dst, rs):
        piece = pl.ds(pl.multiple_of(relay_strip * STRIP, STRIP), STRIP)
        return remote(
            relayed.at[kind], dst.at[piece], r_ss.at[kind], rs.at[relay_strip * STRIP // SLICE],
            at(0, 0, 0, target_z[kind // 2]),
        )

    def relay_own(kind, src, dst, rs):
        return remote(src.at[strip(0)], dst.at[strip(0)], r_ss.at[kind], rs.at[0], at(0, 0, 0, target_z[1]))

    def relay(kind, dst, rs, when):
        through = is_relay if kind < 2 else is_third

        @pl.when(through & when)
        def _():
            remote(relayed.at[kind], relayed.at[kind], r_ss.at[kind], r_rs.at[kind], up).wait_recv()
            relay_copy(kind, dst, rs).start()

        if kind >= 2:
            @pl.when(is_second & when)
            def _():
                relay_own(kind, t_ref if kind == 2 else img_ref, dst, rs).start()

    def relay_end(kind, dst, rs):
        @pl.when(is_relay)
        def _():
            relay_copy(kind, dst, rs).wait_send()

    def text_hop(hop, k, source):
        return (source.at[chunk(k)], tx.at[hop, chunk(k)], t_ss.at[hop, k], t_rs.at[hop, k])

    def image_hop(hop, k, source):
        return (source.at[chunk(k)], ix.at[hop, chunk(k)], i_ss.at[hop, k], i_rs.at[hop, k])

    def after_hop(args, kind, k):
        src, dst, ss, rs = args
        return send_after(src, dst, kind, ss, rs, k, (t_ref, img_ref)[kind % 2])

    hop1 = [after_hop(text_hop(0, k, t_ref), 0, k) for k in range(CHUNKS)]
    second_start(t_ref, 2)
    relay(0, tx.at[0], t_rs.at[0], zh == 0)
    relay(2, tx.at[2], t_rs.at[2], zh == 0)

    loads[1].wait()
    loads[2].wait()
    for k in range(3):
        cols = pl.ds(k * 384, 384)
        proj_ref[:, cols] = dot(a_ref[...], w_ref[:, cols])
    unit, img_inverse = unit_rows(proj_ref[...])
    img_ref[...] = unit.astype(BF16)
    i_hop1 = [after_hop(image_hop(0, k, img_ref), 1, k) for k in range(CHUNKS)]
    second_start(img_ref, 3)
    relay(0, tx.at[0], t_rs.at[0], zh == 1)
    relay(2, tx.at[2], t_rs.at[2], zh == 1)

    multiplier = mult_ref[0]
    bias = bias_ref[0]

    def txt_of(raw):
        return unit_rows(raw.astype(F32))[0].astype(BF16)

    rows = lax.broadcasted_iota(jnp.int32, (ROWS, ROWS), 0)
    cols = lax.broadcasted_iota(jnp.int32, (ROWS, ROWS), 1)
    positive = jnp.where(rows == cols, 1.0, 0.0).astype(F32)

    def scaled_of(left_rows, right_rows, own):
        logits = multiplier * dot(left_rows, right_rows, 1, 1) + bias
        weight = jax.nn.sigmoid(logits)
        if own:
            weight = weight - positive
        return (multiplier * weight).astype(BF16)

    def image_pair(raw, own):
        txt_b = txt_of(raw)
        term = dot(scaled_of(img_ref[...], txt_b, own), txt_b)
        if own:
            igrad[...] = term
        else:
            igrad[...] += term

    hop2 = []
    for k in range(CHUNKS):
        hop1[k].wait_recv()
        hop2.append(send(*text_hop(1, k, tx.at[0]), up))
    pl.semaphore_wait(near_y, 2)
    pl.semaphore_wait(near_z, 2)
    tell(mid_y, two_column)
    tell(mid_z, two_tower)
    loads[3].wait()
    for k in range(NX * NC):
        at_all[k] = dot(order_ref[pl.ds(k * BLOCK, BLOCK), :], a_ref[...], 1, 1).astype(BF16)
    at_got[0, :, :128] = at_all[x * 2 + c]
    a_copies = []
    for k in range(NX):
        for dc in range(NC):
            slot = k * 2 + dc
            if slot == 0:
                continue
            to_x, to_c = (x + k) % NX, (c + dc) % 2
            a_copies.append(
                send(
                    at_all.at[to_x * 2 + to_c], at_got.at[k, :, pl.ds(dc * 128, 128)],
                    a_ss.at[slot], a_rs.at[slot], at(to_c, to_x, y, z),
                )
            )
    relay(1, ix.at[0], i_rs.at[0], c >= 0)
    relay(3, ix.at[2], i_rs.at[2], c >= 0)
    image_pair(t_ref[...], True)
    image_pair(tx[0], False)
    for q in range(PARTS):
        for half in range(2):
            pieces[q, :, half * PIECE + NT * OWN : (half + 1) * PIECE, :] = jnp.zeros(
                (NY, PIECE - NT * OWN, 128), F32
            )
    hop3 = []
    for k in range(CHUNKS):
        hop2[k].wait_recv()
        hop3.append(after_hop(text_hop(2, k, tx.at[1]), 2, k))
    pl.semaphore_wait(mid_y, 2)
    pl.semaphore_wait(mid_z, 2)
    tell(far_sem, two_tower)
    image_pair(tx[1], False)
    for k in range(CHUNKS):
        hop3[k].wait_recv()
    image_pair(tx[2], False)

    unit, img_inverse = unit_rows(proj_ref[...])
    grad = igrad[...]
    proj_grad = (
        (grad - unit * jnp.sum(unit * grad, axis=1, keepdims=True)) * img_inverse
    ).astype(BF16)
    for q in range(PARTS):
        p_got[0, q, :ROWS] = proj_grad[:, q * COLS : (q + 1) * COLS]

    first, second = pl.ds(0, HALF), pl.ds(HALF, HALF)
    own_rows, partner_rows = pl.ds(0, ROWS), pl.ds(ROWS, ROWS)
    p_copies, q_copies, f_copies, y_copies = {}, {}, {}, {}

    def p_send(k, q, half, device):
        rows_ = (first, second)[half]
        p_copies[k, q, half] = send(
            p_got.at[0, q, rows_], p_got.at[k, q, rows_], p_ss.at[k, q, half], p_rs.at[k, q, half], device
        )

    def q_send(k, q):
        q_copies[k, q] = send(
            p_got.at[k, q, own_rows], p_got.at[k, q, partner_rows], q_ss.at[k, q], q_rs.at[k, q], partner
        )

    for q in range(PARTS):
        p_send(1, q, 0, right)
        p_send(3, q, 1, left)
        p_send(1, q, 1, right)
        p_send(3, q, 0, left)
    for q in range(PARTS):
        q_send(0, q)

    def forward(q):
        p_copies[1, q, 0].wait_recv()
        f_copies[q, 0] = send(
            p_got.at[1, q, first], p_got.at[2, q, first], f_ss.at[q, 0], p_rs.at[2, q, 0], right
        )
        p_copies[3, q, 1].wait_recv()
        f_copies[q, 1] = send(
            p_got.at[3, q, second], p_got.at[2, q, second], f_ss.at[q, 1], p_rs.at[2, q, 1], left
        )

    def over_x(q):
        p_copies[1, q, 1].wait_recv()
        q_send(1, q)
        p_copies[3, q, 0].wait_recv()
        q_send(3, q)
        f_copies[q, 0].wait_recv()
        f_copies[q, 1].wait_recv()
        q_send(2, q)
        for k in range(NX):
            q_copies[k, q].wait_recv()
        acc = dot(at_got[0], p_got[0, q])
        for k in range(1, NX):
            acc = acc + dot(at_got[k], p_got[k, q])
        out[...] = acc
        for to_y in range(NY):
            for half in range(2):
                for j in range(NT):
                    source = (to_y * 2 + half) * OWN
                    target = half * PIECE + j * OWN
                    pieces[q, to_y, target : target + OWN, :] = out[
                        source : source + OWN, j * 128 : (j + 1) * 128
                    ]
        ysend[q] = pieces[q].astype(BF16)
        for k in (4, 3, 5, 2, 6, 1, 7):
            to_y = (y + k) % NY
            y_copies[q, k] = send(
                ysend.at[q, to_y], ygot.at[q, k], y_ss.at[q, k], y_rs.at[q, k], at(c, x, to_y, z)
            )

    z_copies = {}

    def over_y(q):
        total = pieces[q, y]
        for k in (1, 7, 2, 6, 3, 5, 4):
            y_copies[q, k].wait_recv()
            total = total + ygot[q, k].astype(F32)
        zsend[q, 0] = total[:PIECE].astype(BF16)
        zsend[q, 1] = total[PIECE:].astype(BF16)
        zgot[q, z] = zsend[q, zh]
        for k in (6, 5, 7, 4, 8, 3, 9, 2, 10, 1, 11):
            to_z = (z + k) % NZ
            z_copies[q, k] = send(
                zsend.at[q, to_z // NG], zgot.at[q, z], z_ss.at[q, k], z_rs.at[q, k], at(c, x, y, to_z)
            )

    for copy in a_copies:
        copy.wait_recv()
    forward(0)
    forward(1)
    i_hop2 = []
    for k in range(CHUNKS):
        i_hop1[k].wait_recv()
        i_hop2.append(send(*image_hop(1, k, ix.at[0]), up))
    over_x(0)
    forward(2)
    over_x(1)
    pl.semaphore_wait(far_sem, 2)
    i_hop3 = []
    for k in range(CHUNKS):
        i_hop2[k].wait_recv()
        i_hop3.append(after_hop(image_hop(2, k, ix.at[1]), 3, k))
    over_y(0)
    over_x(2)
    over_y(1)
    over_y(2)

    txt_b = txt_of(tx[2])

    def text_pair(image, own):
        return dot(scaled_of(txt_b, image, own), image)

    tsum[...] = text_pair(img_ref[...], False)
    tsum[...] += text_pair(ix[0], False)
    tsum[...] += text_pair(ix[1], False)

    for k in range(CHUNKS):
        i_hop3[k].wait_recv()
    tsum[...] += text_pair(ix[2], True)
    grad = tsum[...]
    unit_txt, txt_inverse = unit_rows(tx[2].astype(F32))
    tgrad_ref[...] = (
        (grad - unit_txt * jnp.sum(unit_txt * grad, axis=1, keepdims=True)) * txt_inverse
    ).astype(BF16)

    for q in range(PARTS):
        for k in (1, 11, 2, 10, 3, 9, 4, 8, 5, 7, 6):
            z_copies[q, k].wait_recv()
        total = zgot[q, 0].astype(F32)
        for k in range(1, NZ):
            total = total + zgot[q, k].astype(F32)
        final[...] = total
        for j in range(NT):
            target = (q * NT + j) * 128
            head_ref[:, target : target + 128] = final[j * OWN : (j + 1) * OWN, :].astype(BF16)

    for copy in started:
        copy.wait_send()
    relay_end(0, tx.at[0], t_rs.at[0])
    relay_end(1, ix.at[0], i_rs.at[0])
    relay_end(2, tx.at[2], t_rs.at[2])
    second_end(t_ref, 2)
    second_end(img_ref, 3)

    @pl.when(jnp.logical_not(is_source))
    def _():
        for copy in kept:
            copy.wait_send()

    relay_end(3, ix.at[2], i_rs.at[2])


def row_order():
    source = np.arange(D).reshape(2, NY, NX, NC, OWN).transpose(2, 3, 1, 0, 4).reshape(-1)
    order = np.zeros((D, D), np.float32)
    order[np.arange(D), source] = 1.0
    return order


def local(descriptors, captions, weights, multiplier, bias):
    order = jnp.asarray(row_order(), BF16)
    vmem = pl.BlockSpec(memory_space=pltpu.VMEM)
    smem = pl.BlockSpec(memory_space=pltpu.SMEM)
    hbm = pl.BlockSpec(memory_space=pltpu.HBM)
    dma = pltpu.SemaphoreType.DMA
    head, text = pl.pallas_call(
        kernel,
        out_shape=(
            jax.ShapeDtypeStruct((OWN, D), BF16),
            jax.ShapeDtypeStruct((ROWS, D), BF16),
        ),
        in_specs=[smem, smem, hbm, hbm, hbm, hbm],
        out_specs=(vmem, vmem),
        scratch_shapes=[
            pltpu.VMEM((ROWS, D), BF16),
            pltpu.VMEM((ROWS, D), BF16),
            pltpu.VMEM((D, D), BF16),
            pltpu.VMEM((D, D), BF16),
            pltpu.VMEM((ROWS, D), F32),
            pltpu.VMEM((ROWS, D), BF16),
            pltpu.VMEM((3, ROWS, D), BF16),
            pltpu.VMEM((3, ROWS, D), BF16),
            pltpu.VMEM((4, STRIP, D), BF16),
            pltpu.VMEM((ROWS, D), F32),
            pltpu.VMEM((ROWS, D), F32),
            pltpu.VMEM((NX * NC, BLOCK, ROWS), BF16),
            pltpu.VMEM((NX, BLOCK, NC * ROWS), BF16),
            pltpu.VMEM((NX, PARTS, NC * ROWS, COLS), BF16),
            pltpu.VMEM((BLOCK, COLS), F32),
            pltpu.VMEM((PARTS, NY, 2 * PIECE, 128), F32),
            pltpu.VMEM((PARTS, NY, 2 * PIECE, 128), BF16),
            pltpu.VMEM((PARTS, NY, 2 * PIECE, 128), BF16),
            pltpu.VMEM((PARTS, 2, PIECE, 128), BF16),
            pltpu.VMEM((PARTS, NZ, PIECE, 128), BF16),
            pltpu.VMEM((PIECE, 128), F32),
            pltpu.SemaphoreType.REGULAR,
            pltpu.SemaphoreType.REGULAR,
            pltpu.SemaphoreType.REGULAR,
            pltpu.SemaphoreType.REGULAR,
            pltpu.SemaphoreType.REGULAR,
            dma((4,)),
            dma((2, len(RELAYS))),
            dma((3, CHUNKS)),
            dma((3, CHUNKS)),
            dma((3, CHUNKS)),
            dma((3, CHUNKS)),
            dma((4,)),
            dma((4,)),
            dma((NX * NC,)),
            dma((NX * NC,)),
            dma((NX, PARTS, 2)),
            dma((NX, PARTS, 2)),
            dma((PARTS, 2)),
            dma((NX, PARTS)),
            dma((NX, PARTS)),
            dma((PARTS, NY)),
            dma((PARTS, NY)),
            dma((PARTS, NZ)),
            dma((PARTS, NZ)),
        ],
        compiler_params=pltpu.CompilerParams(
            collective_id=0, has_side_effects=True, vmem_limit_bytes=60 * 1024 * 1024
        ),
        name="window_grads",
    )(multiplier, bias, descriptors, captions, weights, order)
    return head, text


def solution(mesh):
    in_specs = (P(("blk", "group"), None), P(("blk", "group"), None), P(), P(), P())
    out_specs = (P("blk", None), P(("blk", "group"), None))
    return jax.shard_map(local, mesh=mesh, in_specs=in_specs, out_specs=out_specs, check_vma=False)
```

```python
import jax
import jax.numpy as jnp
import numpy as np
from jax import lax
from jax.experimental import pallas as pl
from jax.experimental.pallas import tpu as pltpu
from jax.sharding import PartitionSpec as P

MESH = pl.DeviceIdType.MESH
EPS = 1e-06
NC, NX, NY, NZ, NG = 2, 4, 8, 12, 6
ROWS, D = 128, 1152
OWN = 9
BLOCK = 144
COLS = 384
PARTS = 3
PIECE = 32
CHUNKS = 2
NT = COLS // 128
SLICE = ROWS // CHUNKS
HALF = ROWS // 2
RELAYS = ((0, 3, 7), (1, 0, 7), (1, 3, 0), (1, 0, 0), (1, 2, 7), (1, 2, 0), (1, 3, 6), (1, 0, 6))
IMAGE_RELAYS = ((0, 3, 7), (1, 1, 7), (1, 1, 0), (1, 3, 1), (1, 0, 1), (1, 2, 6), (1, 2, 1), (1, 1, 6))
STRIP = ROWS // len(RELAYS)
F32, BF16 = jnp.float32, jnp.bfloat16


def dot(a, b, ca=1, cb=0):
    return lax.dot_general(a, b, (((ca,), (cb,)), ((), ())), preferred_element_type=F32)


def unit_rows(wide):
    inverse = lax.rsqrt(jnp.sum(wide * wide, axis=1, keepdims=True) + EPS)
    return wide * inverse, inverse


def kernel(
    mult_ref, bias_ref, a_hbm, t_hbm, w_hbm, order_hbm,
    head_ref, tgrad_ref,
    a_ref, t_ref, w_ref, order_ref, proj_ref, img_ref, tx, ix, relayed, igrad, tsum,
    at_all, at_got, p_got, out, pieces, ysend, ygot, zsend, zgot, final,
    near_y, mid_y, near_z, mid_z, far_sem, local_sem, s_ss, t_ss, t_rs, i_ss, i_rs, r_ss, r_rs, a_ss, a_rs,
    p_ss, p_rs, f_ss, q_ss, q_rs, y_ss, y_rs, z_ss, z_rs,
):
    b = lax.axis_index("blk")
    g = lax.axis_index("group")
    c, x, y, zh = b % 2, (b // 2) % NX, (b // 8) % NY, b // 64
    z = zh * NG + g

    def at(c_, x_, y_, z_):
        return ((z_ // NG) * 64 + y_ * 8 + x_ * 2 + c_, z_ % NG)

    after = ((b + 1) % 128, g)
    before = ((b + 127) % 128, g)
    up = (b, (g + 1) % NG)
    down = (b, (g + 5) % NG)
    partner = at(1 - c, x, y, z)
    right = at(c, (x + 1) % NX, y, z)
    left = at(c, (x + 3) % NX, y, z)

    far_z = (z + 6) % NZ
    is_source = (c == 1) & (x == 3) & (y == 7)
    is_target = (c == 0) & (x == 0) & (y == 0)
    is_second = (c == 0) & (x == 3) & (y == 7)
    place = (y * NX + x) * NC + c
    carries = []
    for spots in (RELAYS, IMAGE_RELAYS):
        third, number = b < 0, 0
        for i, (c_, x_, y_) in enumerate(spots):
            here = place == (y_ * NX + x_) * NC + c_
            if i:
                third = third | here
            number = number + i * here.astype(jnp.int32)
        carries.append((third, number))
    is_third = carries[0][0] | carries[1][0]
    is_relay = is_second | is_third
    other = (1 - zh) * NG
    target_z = (far_z, other + (g + 1) % NG)
    origin_z = (far_z, other + (g + 5) % NG)

    def relays_at(z_, kind):
        return [at(*spot, z_) for spot in (RELAYS, IMAGE_RELAYS)[kind % 2]]

    loads = []
    for i, (src, dst) in enumerate(
        ((t_hbm, t_ref), (a_hbm, a_ref), (w_hbm, w_ref), (order_hbm, order_ref))
    ):
        load = pltpu.make_async_copy(src, dst, local_sem.at[i])
        load.start()
        loads.append(load)

    ring = [at(core, (x + k) % NX, y, z) for k in range(1, NX) for core in range(NC)]
    column = [at(c, x, (y + k) % NY, z) for k in (1, 7)]
    tower = [at(c, x, y, (z + k) % NZ) for k in (1, 11)]
    greeted = [up, down, partner] + ring + column + tower
    barrier = pltpu.get_barrier_semaphore()

    def greet(device):
        pl.semaphore_signal(barrier, inc=1, device_id=device, device_id_type=MESH)

    for device in greeted:
        greet(device)

    @pl.when(jnp.logical_not(is_source))
    def _():
        greet(after)

    @pl.when(jnp.logical_not(is_target))
    def _():
        greet(before)

    @pl.when(is_relay)
    def _():
        greet(at(1, 3, 7, z))

    @pl.when(is_third)
    def _():
        greet(at(0, 3, 7, z))

    @pl.when(is_target)
    def _():
        for z_ in origin_z:
            for device in relays_at(z_, 0) + relays_at(z_, 1)[1:]:
                greet(device)

    loads[0].wait()
    def one(flag):
        return flag.astype(jnp.int32)

    expected = len(greeted) + 2 + 2 * (len(RELAYS) - 1) * one(is_source) - one(is_target)
    expected = expected + 2 * one(is_relay) + 2 * (len(RELAYS) - 1) * one(is_second)
    pl.semaphore_wait(barrier, expected)

    def tell(sem, devices):
        for device in devices:
            pl.semaphore_signal(sem, inc=1, device_id=device, device_id_type=MESH)

    two_column = [at(c, x, (y + k) % NY, z) for k in (2, 6)]
    two_tower = [at(c, x, y, (z + k) % NZ) for k in (2, 10)]
    tell(near_y, column)
    tell(near_z, tower)

    started, kept = [], []

    def remote(src, dst, ss, rs, device):
        return pltpu.make_async_remote_copy(
            src_ref=src, dst_ref=dst, send_sem=ss, recv_sem=rs, device_id=device, device_id_type=MESH
        )

    def send(src, dst, ss, rs, device):
        copy = remote(src, dst, ss, rs, device)
        copy.start()
        started.append(copy)
        return copy

    def strip(i):
        return pl.ds(i * STRIP, STRIP)

    def chunk(k):
        return pl.ds(k * SLICE, SLICE)

    def send_after(src, dst, kind, ss, rs, k, whole):
        direct = remote(src, dst, ss, rs, after)
        if kind >= 2:
            kept.append(direct)
        else:
            started.append(direct)

            @pl.when(is_source)
            def _():
                for i in range(k * SLICE // STRIP, (k + 1) * SLICE // STRIP):
                    remote(
                        whole.at[strip(i)], relayed.at[kind], ss, r_rs.at[kind], relays_at(z, kind)[i]
                    ).start()

        @pl.when(jnp.logical_not(is_source))
        def _():
            direct.start()

        return direct

    def second_copies(src, kind):
        return [
            remote(src.at[strip(i)], relayed.at[kind], s_ss.at[kind - 2, i], r_rs.at[kind], relays_at(z, kind)[i])
            for i in range(1, len(RELAYS))
        ]

    def second_start(src, kind):
        @pl.when(is_second)
        def _():
            for copy in second_copies(src, kind):
                copy.start()

    def second_end(src, kind):
        @pl.when(is_second)
        def _():
            for copy in second_copies(src, kind):
                copy.wait_send()

    def relay_copy(kind, dst, rs):
        relay_strip = carries[kind % 2][1]
        piece = pl.ds(pl.multiple_of(relay_strip * STRIP, STRIP), STRIP)
        return remote(
            relayed.at[kind], dst.at[piece], r_ss.at[kind], rs.at[relay_strip * STRIP // SLICE],
            at(0, 0, 0, target_z[kind // 2]),
        )

    def relay_own(kind, src, dst, rs):
        return remote(src.at[strip(0)], dst.at[strip(0)], r_ss.at[kind], rs.at[0], at(0, 0, 0, target_z[1]))

    def relay(kind, dst, rs, when):
        third = carries[kind % 2][0]
        through = (is_second | third) if kind < 2 else third

        @pl.when(through & when)
        def _():
            remote(relayed.at[kind], relayed.at[kind], r_ss.at[kind], r_rs.at[kind], up).wait_recv()
            relay_copy(kind, dst, rs).start()

        if kind >= 2:
            @pl.when(is_second & when)
            def _():
                relay_own(kind, t_ref if kind == 2 else img_ref, dst, rs).start()

    def relay_end(kind, dst, rs):
        @pl.when(is_second | carries[kind % 2][0])
        def _():
            relay_copy(kind, dst, rs).wait_send()

    def text_hop(hop, k, source):
        return (source.at[chunk(k)], tx.at[hop, chunk(k)], t_ss.at[hop, k], t_rs.at[hop, k])

    def image_hop(hop, k, source):
        return (source.at[chunk(k)], ix.at[hop, chunk(k)], i_ss.at[hop, k], i_rs.at[hop, k])

    def after_hop(args, kind, k):
        src, dst, ss, rs = args
        return send_after(src, dst, kind, ss, rs, k, (t_ref, img_ref)[kind % 2])

    hop1 = [after_hop(text_hop(0, k, t_ref), 0, k) for k in range(CHUNKS)]
    second_start(t_ref, 2)
    relay(0, tx.at[0], t_rs.at[0], zh == 0)
    relay(2, tx.at[2], t_rs.at[2], zh == 0)

    loads[1].wait()
    loads[2].wait()
    for k in range(3):
        cols = pl.ds(k * 384, 384)
        proj_ref[:, cols] = dot(a_ref[...], w_ref[:, cols])
    unit, img_inverse = unit_rows(proj_ref[...])
    img_ref[...] = unit.astype(BF16)
    i_hop1 = [after_hop(image_hop(0, k, img_ref), 1, k) for k in range(CHUNKS)]
    second_start(img_ref, 3)
    relay(0, tx.at[0], t_rs.at[0], zh == 1)
    relay(2, tx.at[2], t_rs.at[2], zh == 1)

    multiplier = mult_ref[0]
    bias = bias_ref[0]

    def txt_of(raw):
        return unit_rows(raw.astype(F32))[0].astype(BF16)

    rows = lax.broadcasted_iota(jnp.int32, (ROWS, ROWS), 0)
    cols = lax.broadcasted_iota(jnp.int32, (ROWS, ROWS), 1)
    positive = jnp.where(rows == cols, 1.0, 0.0).astype(F32)

    def scaled_of(left_rows, right_rows, own):
        logits = multiplier * dot(left_rows, right_rows, 1, 1) + bias
        weight = jax.nn.sigmoid(logits)
        if own:
            weight = weight - positive
        return (multiplier * weight).astype(BF16)

    def image_pair(raw, own):
        txt_b = txt_of(raw)
        term = dot(scaled_of(img_ref[...], txt_b, own), txt_b)
        if own:
            igrad[...] = term
        else:
            igrad[...] += term

    hop2 = []
    for k in range(CHUNKS):
        hop1[k].wait_recv()
        hop2.append(send(*text_hop(1, k, tx.at[0]), up))
    pl.semaphore_wait(near_y, 2)
    pl.semaphore_wait(near_z, 2)
    tell(mid_y, two_column)
    tell(mid_z, two_tower)
    relay(1, ix.at[0], i_rs.at[0], c >= 0)
    relay(3, ix.at[2], i_rs.at[2], c >= 0)
    image_pair(t_ref[...], True)
    image_pair(tx[0], False)
    loads[3].wait()
    for k in range(NX * NC):
        at_all[k] = dot(order_ref[pl.ds(k * BLOCK, BLOCK), :], a_ref[...], 1, 1).astype(BF16)
    at_got[0, :, :128] = at_all[x * 2 + c]
    a_copies = []
    for k in range(NX):
        for dc in range(NC):
            slot = k * 2 + dc
            if slot == 0:
                continue
            to_x, to_c = (x + k) % NX, (c + dc) % 2
            a_copies.append(
                send(
                    at_all.at[to_x * 2 + to_c], at_got.at[k, :, pl.ds(dc * 128, 128)],
                    a_ss.at[slot], a_rs.at[slot], at(to_c, to_x, y, z),
                )
            )
    for q in range(PARTS):
        for half in range(2):
            pieces[q, :, half * PIECE + NT * OWN : (half + 1) * PIECE, :] = jnp.zeros(
                (NY, PIECE - NT * OWN, 128), F32
            )
    hop3 = []
    for k in range(CHUNKS):
        hop2[k].wait_recv()
        hop3.append(after_hop(text_hop(2, k, tx.at[1]), 2, k))
    pl.semaphore_wait(mid_y, 2)
    pl.semaphore_wait(mid_z, 2)
    tell(far_sem, two_tower)
    image_pair(tx[1], False)
    for k in range(CHUNKS):
        hop3[k].wait_recv()
    image_pair(tx[2], False)

    unit, img_inverse = unit_rows(proj_ref[...])
    grad = igrad[...]
    proj_grad = (
        (grad - unit * jnp.sum(unit * grad, axis=1, keepdims=True)) * img_inverse
    ).astype(BF16)
    for q in range(PARTS):
        p_got[0, q, :ROWS] = proj_grad[:, q * COLS : (q + 1) * COLS]

    first, second = pl.ds(0, HALF), pl.ds(HALF, HALF)
    own_rows, partner_rows = pl.ds(0, ROWS), pl.ds(ROWS, ROWS)
    p_copies, q_copies, f_copies, y_copies = {}, {}, {}, {}

    def p_send(k, q, half, device):
        rows_ = (first, second)[half]
        p_copies[k, q, half] = send(
            p_got.at[0, q, rows_], p_got.at[k, q, rows_], p_ss.at[k, q, half], p_rs.at[k, q, half], device
        )

    def q_send(k, q):
        q_copies[k, q] = send(
            p_got.at[k, q, own_rows], p_got.at[k, q, partner_rows], q_ss.at[k, q], q_rs.at[k, q], partner
        )

    for q in range(PARTS):
        p_send(1, q, 0, right)
        p_send(3, q, 1, left)
        p_send(1, q, 1, right)
        p_send(3, q, 0, left)
    for q in range(PARTS):
        q_send(0, q)

    def forward(q):
        p_copies[1, q, 0].wait_recv()
        f_copies[q, 0] = send(
            p_got.at[1, q, first], p_got.at[2, q, first], f_ss.at[q, 0], p_rs.at[2, q, 0], right
        )
        p_copies[3, q, 1].wait_recv()
        f_copies[q, 1] = send(
            p_got.at[3, q, second], p_got.at[2, q, second], f_ss.at[q, 1], p_rs.at[2, q, 1], left
        )

    def over_x(q):
        p_copies[1, q, 1].wait_recv()
        q_send(1, q)
        p_copies[3, q, 0].wait_recv()
        q_send(3, q)
        f_copies[q, 0].wait_recv()
        f_copies[q, 1].wait_recv()
        q_send(2, q)
        for k in range(NX):
            q_copies[k, q].wait_recv()
        acc = dot(at_got[0], p_got[0, q])
        for k in range(1, NX):
            acc = acc + dot(at_got[k], p_got[k, q])
        out[...] = acc
        for to_y in range(NY):
            for half in range(2):
                for j in range(NT):
                    source = (to_y * 2 + half) * OWN
                    target = half * PIECE + j * OWN
                    pieces[q, to_y, target : target + OWN, :] = out[
                        source : source + OWN, j * 128 : (j + 1) * 128
                    ]
        ysend[q] = pieces[q].astype(BF16)
        for k in (4, 3, 5, 2, 6, 1, 7):
            to_y = (y + k) % NY
            y_copies[q, k] = send(
                ysend.at[q, to_y], ygot.at[q, k], y_ss.at[q, k], y_rs.at[q, k], at(c, x, to_y, z)
            )

    z_copies = {}

    def over_y(q):
        total = pieces[q, y]
        for k in (1, 7, 2, 6, 3, 5, 4):
            y_copies[q, k].wait_recv()
            total = total + ygot[q, k].astype(F32)
        zsend[q, 0] = total[:PIECE].astype(BF16)
        zsend[q, 1] = total[PIECE:].astype(BF16)
        zgot[q, z] = zsend[q, zh]
        for k in (6, 5, 7, 4, 8, 3, 9, 2, 10, 1, 11):
            to_z = (z + k) % NZ
            z_copies[q, k] = send(
                zsend.at[q, to_z // NG], zgot.at[q, z], z_ss.at[q, k], z_rs.at[q, k], at(c, x, y, to_z)
            )

    for copy in a_copies:
        copy.wait_recv()
    forward(0)
    forward(1)
    i_hop2 = []
    for k in range(CHUNKS):
        i_hop1[k].wait_recv()
        i_hop2.append(send(*image_hop(1, k, ix.at[0]), up))
    over_x(0)
    forward(2)
    over_x(1)
    pl.semaphore_wait(far_sem, 2)
    i_hop3 = []
    for k in range(CHUNKS):
        i_hop2[k].wait_recv()
        i_hop3.append(after_hop(image_hop(2, k, ix.at[1]), 3, k))
    over_y(0)
    over_x(2)
    over_y(1)
    over_y(2)

    txt_b = txt_of(tx[2])

    def text_pair(image, own):
        return dot(scaled_of(txt_b, image, own), image)

    tsum[...] = text_pair(img_ref[...], False)
    tsum[...] += text_pair(ix[0], False)
    tsum[...] += text_pair(ix[1], False)

    for k in range(CHUNKS):
        i_hop3[k].wait_recv()
    tsum[...] += text_pair(ix[2], True)
    grad = tsum[...]
    unit_txt, txt_inverse = unit_rows(tx[2].astype(F32))
    tgrad_ref[...] = (
        (grad - unit_txt * jnp.sum(unit_txt * grad, axis=1, keepdims=True)) * txt_inverse
    ).astype(BF16)

    for q in range(PARTS):
        for k in (1, 11, 2, 10, 3, 9, 4, 8, 5, 7, 6):
            z_copies[q, k].wait_recv()
        total = zgot[q, 0].astype(F32)
        for k in range(1, NZ):
            total = total + zgot[q, k].astype(F32)
        final[...] = total
        for j in range(NT):
            target = (q * NT + j) * 128
            head_ref[:, target : target + 128] = final[j * OWN : (j + 1) * OWN, :].astype(BF16)

    for copy in started:
        copy.wait_send()
    relay_end(0, tx.at[0], t_rs.at[0])
    relay_end(1, ix.at[0], i_rs.at[0])
    relay_end(2, tx.at[2], t_rs.at[2])
    second_end(t_ref, 2)
    second_end(img_ref, 3)

    @pl.when(jnp.logical_not(is_source))
    def _():
        for copy in kept:
            copy.wait_send()

    relay_end(3, ix.at[2], i_rs.at[2])


def row_order():
    source = np.arange(D).reshape(2, NY, NX, NC, OWN).transpose(2, 3, 1, 0, 4).reshape(-1)
    order = np.zeros((D, D), np.float32)
    order[np.arange(D), source] = 1.0
    return order


def local(descriptors, captions, weights, multiplier, bias):
    order = jnp.asarray(row_order(), BF16)
    vmem = pl.BlockSpec(memory_space=pltpu.VMEM)
    smem = pl.BlockSpec(memory_space=pltpu.SMEM)
    hbm = pl.BlockSpec(memory_space=pltpu.HBM)
    dma = pltpu.SemaphoreType.DMA
    head, text = pl.pallas_call(
        kernel,
        out_shape=(
            jax.ShapeDtypeStruct((OWN, D), BF16),
            jax.ShapeDtypeStruct((ROWS, D), BF16),
        ),
        in_specs=[smem, smem, hbm, hbm, hbm, hbm],
        out_specs=(vmem, vmem),
        scratch_shapes=[
            pltpu.VMEM((ROWS, D), BF16),
            pltpu.VMEM((ROWS, D), BF16),
            pltpu.VMEM((D, D), BF16),
            pltpu.VMEM((D, D), BF16),
            pltpu.VMEM((ROWS, D), F32),
            pltpu.VMEM((ROWS, D), BF16),
            pltpu.VMEM((3, ROWS, D), BF16),
            pltpu.VMEM((3, ROWS, D), BF16),
            pltpu.VMEM((4, STRIP, D), BF16),
            pltpu.VMEM((ROWS, D), F32),
            pltpu.VMEM((ROWS, D), F32),
            pltpu.VMEM((NX * NC, BLOCK, ROWS), BF16),
            pltpu.VMEM((NX, BLOCK, NC * ROWS), BF16),
            pltpu.VMEM((NX, PARTS, NC * ROWS, COLS), BF16),
            pltpu.VMEM((BLOCK, COLS), F32),
            pltpu.VMEM((PARTS, NY, 2 * PIECE, 128), F32),
            pltpu.VMEM((PARTS, NY, 2 * PIECE, 128), BF16),
            pltpu.VMEM((PARTS, NY, 2 * PIECE, 128), BF16),
            pltpu.VMEM((PARTS, 2, PIECE, 128), BF16),
            pltpu.VMEM((PARTS, NZ, PIECE, 128), BF16),
            pltpu.VMEM((PIECE, 128), F32),
            pltpu.SemaphoreType.REGULAR,
            pltpu.SemaphoreType.REGULAR,
            pltpu.SemaphoreType.REGULAR,
            pltpu.SemaphoreType.REGULAR,
            pltpu.SemaphoreType.REGULAR,
            dma((4,)),
            dma((2, len(RELAYS))),
            dma((3, CHUNKS)),
            dma((3, CHUNKS)),
            dma((3, CHUNKS)),
            dma((3, CHUNKS)),
            dma((4,)),
            dma((4,)),
            dma((NX * NC,)),
            dma((NX * NC,)),
            dma((NX, PARTS, 2)),
            dma((NX, PARTS, 2)),
            dma((PARTS, 2)),
            dma((NX, PARTS)),
            dma((NX, PARTS)),
            dma((PARTS, NY)),
            dma((PARTS, NY)),
            dma((PARTS, NZ)),
            dma((PARTS, NZ)),
        ],
        compiler_params=pltpu.CompilerParams(
            collective_id=0, has_side_effects=True, vmem_limit_bytes=60 * 1024 * 1024
        ),
        name="window_grads",
    )(multiplier, bias, descriptors, captions, weights, order)
    return head, text


def solution(mesh):
    in_specs = (P(("blk", "group"), None), P(("blk", "group"), None), P(), P(), P())
    out_specs = (P("blk", None), P(("blk", "group"), None))
    return jax.shard_map(local, mesh=mesh, in_specs=in_specs, out_specs=out_specs, check_vma=False)
```
